128 devices in a mesh: slab: 8 (over y, core), grp: 16 (over z, x).
Axes of the slice: x: 4, y: 4, z: 4, core: 2. Of those that a mesh axis runs over, the one named last changes fastest.
Arguments:
- source: bfloat16 [1024, 64, 4096], P(('slab', 'grp')), may hold values from -6 to 6
- momentum: bfloat16 [1024, 64, 4096], P(('slab', 'grp')), may hold values from -6 to 6
- velocity: float32 [1, 3, 64, 128, 64], P(None, None, 'slab', 'grp'), may hold values from -12 to 12
- up_taps: float32 [16], replicated, may hold values from 0.2 to 0.8
- smooth_taps: float32 [17], replicated, may hold values from 0.02 to 0.1
- weights: bfloat16 [2048, 64, 192], P(('slab', 'grp')), may hold values from -0.3 to 1.3
- slot_brick: int32 [128, 16], P('slab'), may hold values from -1 to 127, as said below
Outputs:
- image_out: bfloat16 [2048, 64, 4096], P(('slab', 'grp'))
- momentum_out: bfloat16 [2048, 64, 4096], P(('slab', 'grp'))
The draws below stay inside these ranges and needn't reach their ends.
Inputs may be any that keep to these rules, and one draw needn't show every extreme that they name: `slot_brick`: row r lists, in rising order of owner, the bricks of its slab (numbered within the slab, brick k held by the slab's device k // 8 along grp) that device r reads, then -1. No device reads two bricks of one owner, no brick is read twice, and in every slab some device fills all 16 slots.
All inputs are finite; a program needn't handle non-finite values.
Results may differ from the reference program's by a relative error of at most 0.006.
Values may be sent and summed in bfloat16 or wider, within the bound.
A program may use at most 192 MiB of HBM per device.

```python
import math
import jax
import jax.numpy as jnp
from jax import lax

E = 64
STEPS = 1
OWN = 8
CAP = 16
NBS = 128
BRICKS = 1024
SLOTS = 2048
ZC = 64
YC = 128
XC = 64
N_SLAB = 8
N_GRP = 16


def routing_tables(key):
    half_count = N_GRP // 2
    owner_ids = jnp.arange(N_GRP, dtype=jnp.int32)[:, None]
    turn_ids = jnp.arange(OWN, dtype=jnp.int32)[None, :]
    pair_ids = (owner_ids // 2 + turn_ids) % half_count

    def one_slab(slab_key):
        key_hot, key_side, key_tissue, key_order = jax.random.split(slab_key, 4)
        hot_pair = jax.random.randint(key_hot, (), 0, half_count)
        side_bits = jax.random.randint(key_side, (N_GRP, OWN), 0, 2)
        side_bits = jnp.where(pair_ids == hot_pair, 0, side_bits)
        tissue = (jax.random.randint(key_tissue, (N_GRP, OWN), 0, 20) < 17) | (pair_ids == hot_pair)
        reader_order = jax.random.permutation(key_order, N_GRP).astype(jnp.int32)
        readers = reader_order[2 * pair_ids + side_bits]
        readers = jnp.where(tissue, readers, -1)
        match_table = readers[None, :, :] == jnp.arange(N_GRP, dtype=jnp.int32)[:, None, None]
        from_owner = jnp.any(match_table, axis=2)
        turn_taken = jnp.sum(jnp.where(match_table, turn_ids[None, :, :], 0), axis=2)
        places = jnp.cumsum(from_owner.astype(jnp.int32), axis=1) - 1
        places = jnp.where(from_owner, places, CAP)
        brick_ids = (owner_ids.reshape(1, N_GRP) * OWN + turn_taken).astype(jnp.int32)
        row_ids = jnp.broadcast_to(jnp.arange(N_GRP, dtype=jnp.int32)[:, None], (N_GRP, N_GRP))
        slot_table = jnp.full((N_GRP, CAP), -1, jnp.int32)
        slot_table = slot_table.at[row_ids, places].set(brick_ids, mode='drop')
        return slot_table
    slab_keys = jax.random.split(key, N_SLAB)
    slot_table = jax.vmap(one_slab)(slab_keys)
    return slot_table.reshape(N_SLAB * N_GRP, CAP)


def draw_slot_brick(key, part):
    return routing_tables(key)


def draw_weights(key, part):
    key = jax.random.fold_in(key, 7)
    key_share, key_noise = jax.random.split(key)
    row_ids = jnp.arange(E, dtype=jnp.int32)[:, None, None]
    col_ids = jnp.arange(E, dtype=jnp.int32)[None, None, :]
    share_part = jax.random.uniform(key_share, (SLOTS, E, 3 * STEPS, 1), jnp.float32, 0.1, 0.5)
    diagonal = (col_ids == row_ids).astype(jnp.float32)
    neighbour = (col_ids == jnp.minimum(row_ids + 1, E - 1)).astype(jnp.float32)
    base_rows = (1.0 - share_part) * diagonal + share_part * neighbour
    noise_part = 0.26 * jnp.clip(jax.random.normal(key_noise, (SLOTS, E, 3 * STEPS, E), jnp.float32), -4.0, 4.0)
    return (base_rows + noise_part / math.sqrt(E)).reshape(SLOTS, E, 3 * STEPS * E).astype(jnp.bfloat16)


def level_of(own_key, shape, pieces, low, top_value):
    loudness, own = 1.0, jax.random.fold_in(own_key, 6)
    for position, blocks in pieces:
        draws = jnp.exp(jax.random.uniform(jax.random.fold_in(own, position), (blocks,), jnp.float32, low / len(pieces), top_value / len(pieces)))
        loudness = loudness * jnp.repeat(draws, shape[position] // blocks).reshape([-1 if axis == position else 1 for axis in range(len(shape))])
    return loudness


def noise(rng, extent, width, limit, shards=(), held_as=jnp.bfloat16):
    result = width * jax.random.normal(rng, extent, jnp.float32)
    if shards:
        result = result * level_of(rng, extent, shards, -0.22, 0.18)
    return jnp.clip(result, -limit, limit).astype(held_as)


def setup_inputs(seed: int = 0) -> dict:
    splits = jax.random.split(jax.random.key(seed), 8)
    return {
        "source": noise(splits[0], (BRICKS, E, E * E), 1.0, 6.0, ((0, 128),)),
        "momentum": noise(splits[1], (BRICKS, E, E * E), 1.0, 6.0, ((0, 128),)),
        "velocity": noise(splits[2], (STEPS, 3, ZC, YC, XC), 3.0, 12.0, ((2, 8), (3, 16)), jnp.float32),
        "up_taps": jnp.clip(jax.random.uniform(splits[3], (16,), jnp.float32, 0.2, 0.8), 0.2, 0.8),
        "smooth_taps": jnp.clip(jax.random.uniform(splits[4], (17,), jnp.float32, 0.02, 0.1), 0.02, 0.1),
        "weights": draw_weights(jax.random.fold_in(splits[7], 71), 0),
        "slot_brick": draw_slot_brick(jax.random.fold_in(splits[7], 71), 0),
    }


step_time = 0.5
highest = lax.Precision.HIGHEST
einsum_forms = ("ai,ijk->ajk", "bj,ijk->ibk", "ck,ijk->ijc")


def shape_matrix(up_taps, smooth_taps, brick_edge, window_len):
    row_ids = jnp.arange(brick_edge, dtype=jnp.int32)[:, None, None]
    col_ids = jnp.arange(window_len, dtype=jnp.int32)[None, :, None]
    tap_ids = jnp.arange(17, dtype=jnp.int32)[None, None, :]
    tap_index = row_ids + tap_ids - 8 * col_ids + 12
    inside = (tap_index >= 0) & (tap_index < 16)
    picked = up_taps[jnp.clip(tap_index, 0, 15)]
    weighted = jnp.where(inside, picked * smooth_taps[tap_ids], jnp.zeros_like(picked))
    return jnp.sum(weighted, axis=2)


def difference_matrix(brick_edge):
    row_ids = jnp.arange(brick_edge, dtype=jnp.int32)[:, None]
    col_ids = jnp.arange(brick_edge, dtype=jnp.int32)[None, :]
    lower_id = jnp.maximum(row_ids - 1, 0)
    upper_id = jnp.minimum(row_ids + 1, brick_edge - 1)
    spacing = (upper_id - lower_id).astype(jnp.float32)
    return ((col_ids == upper_id).astype(jnp.float32) - (col_ids == lower_id).astype(jnp.float32)) / spacing


def apply_along(matrix, field, axis_id):
    return jnp.einsum(einsum_forms[axis_id], matrix.astype(jnp.float32), field.astype(jnp.float32), precision=highest)


def pull(brick, matrices):
    first_pass = apply_along(matrices[2], brick, 2).astype(jnp.bfloat16)
    second_pass = apply_along(matrices[1], first_pass, 1).astype(jnp.bfloat16)
    return apply_along(matrices[0], second_pass, 0)


def advance(image_now, moment, matrices, velocity_fine, difference):
    pulled = pull(image_now, matrices)
    rounded = pulled.astype(jnp.bfloat16)
    drift_term = velocity_fine[0] * apply_along(difference, rounded, 0)
    drift_term = drift_term + velocity_fine[1] * apply_along(difference, rounded, 1)
    drift_term = drift_term + velocity_fine[2] * apply_along(difference, rounded, 2)
    image_next = (pulled - step_time * drift_term).astype(jnp.bfloat16)
    carried = pull(moment, matrices)
    spread = apply_along(difference, (velocity_fine[0] * carried).astype(jnp.bfloat16), 0)
    spread = spread + apply_along(difference, (velocity_fine[1] * carried).astype(jnp.bfloat16), 1)
    spread = spread + apply_along(difference, (velocity_fine[2] * carried).astype(jnp.bfloat16), 2)
    moment_next = (carried - step_time * spread).astype(jnp.bfloat16)
    return image_next, moment_next


def fine_velocity(window, matrix):
    first_pass = jnp.einsum("nijk,ck->nijc", window, matrix, precision=highest)
    second_pass = jnp.einsum("nijc,bj->nibc", first_pass, matrix, precision=highest)
    return jnp.einsum("nibc,ai->nabc", second_pass, matrix, precision=highest)


def shoot(image_now, moment, flat_mats, windows, matrix, difference):
    brick_edge = image_now.shape[0]
    section_count = windows.shape[0]
    matrices = flat_mats.reshape(brick_edge, section_count, 3, brick_edge)
    for section_id in range(section_count):
        velocity_fine = fine_velocity(windows[section_id], matrix)
        section_mats = (matrices[:, section_id, 0], matrices[:, section_id, 1], matrices[:, section_id, 2])
        image_now, moment = advance(image_now, moment, section_mats, velocity_fine, difference)
    return image_now, moment


def reference(source, momentum, velocity, up_taps, smooth_taps, weights, slot_brick):
    brick_edge = source.shape[1]
    coarse_len = brick_edge // 8
    window_len = coarse_len + 4
    section_count = velocity.shape[0]
    matrix = shape_matrix(up_taps, smooth_taps, brick_edge, window_len)
    difference = difference_matrix(brick_edge).astype(jnp.bfloat16)
    padded = jnp.pad(velocity, ((0, 0), (0, 0), (2, 2), (2, 2), (2, 2)))
    capacity = slot_brick.shape[1]
    anchor = jnp.zeros((), jnp.int32)
    cube_shape = (brick_edge, brick_edge, brick_edge)

    def one_slot(slot_index):
        device_id = slot_index // capacity
        slab_id = device_id // N_GRP
        brick_id = slot_brick[device_id, slot_index % capacity]
        present = brick_id >= 0
        safe_id = jnp.maximum(brick_id, 0)
        owner_id = safe_id // OWN
        column = safe_id % OWN
        row_id = slab_id * NBS + safe_id
        image_now = source[row_id].reshape(cube_shape)
        moment = momentum[row_id].reshape(cube_shape)
        starts = (anchor, anchor, slab_id * coarse_len, owner_id * coarse_len, column * coarse_len)
        windows = lax.dynamic_slice(padded, starts, (section_count, 3, window_len, window_len, window_len))
        image_now, moment = shoot(image_now, moment, weights[slot_index], windows, matrix, difference)
        image_now = jnp.where(present, image_now, jnp.zeros_like(image_now))
        moment = jnp.where(present, moment, jnp.zeros_like(moment))
        return image_now.reshape(brick_edge, brick_edge * brick_edge), moment.reshape(brick_edge, brick_edge * brick_edge)

    images, moments = lax.map(one_slot, jnp.arange(slot_brick.shape[0] * capacity, dtype=jnp.int32))
    return images, moments
```

```python
import functools

import jax
import jax.numpy as jnp
import numpy as np
from jax import lax
from jax.experimental import pallas as pl
from jax.experimental.pallas import tpu as pltpu
from jax.sharding import PartitionSpec as P

step_time = 0.5
highest = lax.Precision.HIGHEST
edge = 64
rows_z = 4
rows_x = 4
f32 = jnp.float32
bf16 = jnp.bfloat16

PITCH = 72
UNROLL = 4
MESH = pl.DeviceIdType.MESH

NEAR = ((0, 1), (0, 3), (1, 0), (3, 0))
DIAGONAL = ((1, 1), (1, 3), (3, 1), (3, 3))
KNIGHT = ((2, 1), (2, 3), (1, 2), (3, 2))
FAR = ((0, 2), (2, 0), (2, 2))
ORDER = ((0, 0),) + NEAR + DIAGONAL + KNIGHT + FAR
COUNT = len(ORDER)


def shape_matrix(up_taps, smooth_taps, window_len):
    row_ids = jnp.arange(edge, dtype=jnp.int32)[:, None, None]
    col_ids = jnp.arange(window_len, dtype=jnp.int32)[None, :, None]
    tap_ids = jnp.arange(17, dtype=jnp.int32)[None, None, :]
    up_ids = jnp.arange(16, dtype=jnp.int32)[None, None, None, :]
    tap_index = row_ids + tap_ids - 8 * col_ids + 12
    chosen = (tap_index[..., None] == up_ids).astype(f32)
    return jnp.sum(chosen * up_taps * smooth_taps[:, None], axis=(2, 3))


def difference_matrix():
    difference = np.zeros((edge, edge), np.float32)
    for r in range(edge):
        lower, upper = max(r - 1, 0), min(r + 1, edge - 1)
        difference[r, upper] += 1.0 / (upper - lower)
        difference[r, lower] -= 1.0 / (upper - lower)
    return difference


def brick(n, in_ref, a2_ref, a1_ref, a0_ref, t_ref, l_ref, dz_ref, dx_ref, out_ref, s1, s2, s3, s4, s5):
    left = lax.broadcasted_iota(jnp.int32, (1, 128), 1) < edge

    a2 = a2_ref[n]
    none = jnp.zeros_like(a2)
    halves = [jnp.where(left, a2, none), jnp.where(left, none, a2)]
    w2 = jnp.concatenate(
        [jnp.concatenate(p, axis=1) for half in halves for p in ((half, none), (none, half))], axis=0
    )

    def x_pass(h, c):
        pieces = []
        for k in range(4):
            at = pl.ds(pl.multiple_of(h * 512 + k * 128, 128), 128)
            pieces.append(jnp.concatenate([in_ref[0, :, at], in_ref[1, :, at]], axis=1))
        res = jnp.dot(jnp.concatenate(pieces, axis=0), w2, preferred_element_type=f32)
        for k in range(4):
            for p in range(2):
                row = pl.multiple_of((h * 8 + 2 * k + p) * PITCH, 8)
                s1[pl.ds(row, 64), :] = res[k * 64 : (k + 1) * 64, p * 128 : (p + 1) * 128]
        return c

    lax.fori_loop(0, 8, x_pass, 0, unroll=UNROLL)

    def y_pass(h, c):
        cols = [s1[pl.ds(h * 8 + i, 64, stride=PITCH), :].astype(bf16) for i in range(8)]
        res = jnp.dot(a1_ref[n], jnp.concatenate(cols, axis=1), preferred_element_type=f32)
        for i in range(8):
            row = pl.multiple_of((h * 8 + i) * PITCH, 8)
            s2[pl.ds(row, 64), :] = res[:, i * 128 : (i + 1) * 128]
        return c

    lax.fori_loop(0, 8, y_pass, 0, unroll=UNROLL)

    def to_rows(x):
        return jnp.concatenate([x[:, i * 128 : (i + 1) * 128] for i in range(8)], axis=0)

    def to_cols(x):
        return jnp.concatenate([x[i * 64 : (i + 1) * 64] for i in range(8)], axis=1)

    def z_pass(h, c):
        cols = [s2[pl.ds(h * 8 + i, 64, stride=PITCH), :].astype(bf16) for i in range(8)]
        j = to_rows(
            jnp.dot(a0_ref[n], jnp.concatenate(cols, axis=1), preferred_element_type=f32)
        )
        at = pl.ds(pl.multiple_of(h * 16, 16), 80)
        v = jnp.dot(l_ref[...], t_ref[at, :], preferred_element_type=f32)
        vz, vy, vx = v[:, :128], v[:, 128:256], v[:, 256:]
        carry_z = jnp.where(left, j, vz * j).astype(bf16)
        carry_y = jnp.where(left, j, vy * j).astype(bf16)
        carry_x = jnp.where(left, j, vx * j).astype(bf16)
        gz = to_rows(jnp.dot(dz_ref[...], to_cols(carry_z), preferred_element_type=f32))
        pairs = jnp.concatenate(
            [
                jnp.concatenate(
                    [carry_x[(2 * k) * 64 : (2 * k + 1) * 64], carry_x[(2 * k + 1) * 64 : (2 * k + 2) * 64]],
                    axis=1,
                )
                for k in range(4)
            ],
            axis=0,
        )
        gp = jnp.dot(pairs, dx_ref[...], preferred_element_type=f32)
        gx = jnp.concatenate(
            [gp[k * 64 : (k + 1) * 64, p * 128 : (p + 1) * 128] for k in range(4) for p in range(2)],
            axis=0,
        )
        upd = jnp.where(left, vz, 1.0) * gz + jnp.where(left, vx, 1.0) * gx
        row = pl.multiple_of(h * 512, 512)
        s3[pl.ds(row, 512), :] = j - step_time * upd
        s4[pl.ds(row, 512), :] = (0.5 * step_time) * jnp.where(left, vy, 1.0)
        s5[pl.ds(row + 64, 512), :] = carry_y.astype(f32)
        return c

    lax.fori_loop(0, 8, z_pass, 0, unroll=UNROLL)
    s5[0:64, :] = 2.0 * s5[64:128, :] - s5[128:192, :]
    s5[65 * 64 : 66 * 64, :] = 2.0 * s5[64 * 64 : 65 * 64, :] - s5[63 * 64 : 64 * 64, :]

    def finish(h, c):
        for k in range(4):
            o = []
            for p in range(2):
                row = pl.multiple_of(h * 512 + (2 * k + p) * 64, 64)
                diff = s5[pl.ds(row + 128, 64), :] - s5[pl.ds(row, 64), :]
                o.append(s3[pl.ds(row, 64), :] - s4[pl.ds(row, 64), :] * diff)
            at = pl.ds(pl.multiple_of(h * 512 + k * 128, 128), 128)
            img = jnp.where(left, o[0], pltpu.roll(o[1], 64, 1))
            mom = jnp.where(left, pltpu.roll(o[0], 64, 1), o[1])
            out_ref[0, :, at] = img.astype(bf16)
            out_ref[1, :, at] = mom.astype(bf16)
        return c

    lax.fori_loop(0, 8, finish, 0, unroll=UNROLL)


def shoot_kernel(
    picks, cols, owners, src_ref, mom_ref, mid_ref, up_ref, down_ref, x_ref, a2_ref, a1_ref, a0_ref,
    l_ref, dz_ref, dx_ref,
    oimg_ref, omom_ref, arr_ref, inter_ref,
    stage, in_buf, out_buf, plane, halo, t_buf, s1, s2, s3, s4, s5,
    send1, recv1, send2, recv2, vsend, vrecv, in_sem, out_sem,
):
    grp, slab = lax.axis_index("grp"), lax.axis_index("slab")
    my_z, my_x = grp // rows_x, grp % rows_x
    slabs = lax.axis_size("slab")

    def at_offset(dz, dx):
        return {"slab": slab, "grp": lax.rem(my_z + dz, rows_z) * rows_x + lax.rem(my_x + dx, rows_x)}

    def at_slab(step):
        return {"slab": lax.rem(slab + step + slabs, slabs), "grp": grp}

    barrier = pltpu.get_barrier_semaphore()
    peers = [at_offset(d, 0) for d in (1, 2, 3)] + [at_offset(0, d) for d in (1, 2, 3)]
    peers += [at_slab(1), at_slab(-1)]
    for peer in peers:
        pl.semaphore_signal(barrier, inc=1, device_id=peer, device_id_type=MESH)
    pl.semaphore_wait(barrier, len(peers))

    def remote(src, dst, send, recv, device):
        return pltpu.make_async_remote_copy(
            src_ref=src, dst_ref=dst, send_sem=send, recv_sem=recv, device_id=device, device_id_type=MESH
        )

    halos = [
        remote(up_ref, halo.at[0], vsend.at[0], vrecv.at[0], at_slab(1)),
        remote(down_ref, halo.at[1], vsend.at[1], vrecv.at[1], at_slab(-1)),
    ]
    for c in halos:
        c.start()

    first, second = {}, {}
    for n, (dz, dx) in enumerate(ORDER):
        if n == 0:
            continue
        both = dz != 0 and dx != 0
        for f in range(2):
            leg1 = at_offset(dz, 0) if (f == 0) == (dz != 0) or dx == 0 else at_offset(0, dx)
            if not both:
                leg1 = at_offset(dz, dx)
            into = inter_ref.at[n, f] if both else arr_ref.at[n, f]
            first[n, f] = remote(stage.at[n, f], into, send1.at[n, f], recv1.at[n, f], leg1)
            if both:
                leg2 = at_offset(0, dx) if f == 0 else at_offset(dz, 0)
                second[n, f] = remote(
                    inter_ref.at[n, f], arr_ref.at[n, f], send2.at[n, f], recv2.at[n, f], leg2
                )

    def put(n, c):
        stage[n, 0] = src_ref[picks[n]]
        stage[n, 1] = mom_ref[picks[n]]
        return c

    def start(copies, ns):
        for n in ns:
            for f in range(2):
                copies[n, f].start()

    def landed(copies, ns):
        for n in ns:
            for f in range(2):
                copies[n, f].wait_recv()

    near, diagonal, knight = range(1, 5), range(5, 9), range(9, 13)
    lax.fori_loop(1, 9, put, 0)
    start(first, near)
    start(first, diagonal)

    for c in halos:
        c.wait()
    piece = mid_ref[...]
    piece = piece + jnp.where(slab > 0, halo[0], jnp.zeros_like(piece))
    piece = piece + jnp.where(slab < slabs - 1, halo[1], jnp.zeros_like(piece))
    plane[my_x, my_z] = piece
    column = [
        remote(plane.at[my_x, my_z], plane.at[my_x, my_z], vsend.at[1 + d], vrecv.at[1 + d], at_offset(d, 0))
        for d in (1, 2, 3)
    ]
    for c in column:
        c.start()
    lax.fori_loop(9, 16, put, 0)
    for c in column:
        c.wait()
    across = [
        remote(plane.at[my_x], plane.at[my_x], vsend.at[4 + d], vrecv.at[4 + d], at_offset(0, d))
        for d in (1, 2, 3)
    ]
    for c in across:
        c.start()
    lax.fori_loop(0, 1, put, 0)
    for c in across:
        c.wait()

    def window(n):
        owner, last = owners[n], rows_z * rows_x - 1
        before, after = jnp.maximum(owner - 1, 0), jnp.minimum(owner + 1, last)
        pieces = [
            plane[before & 3, before >> 2, 6:8].reshape(32, 256),
            plane[owner & 3, owner >> 2].reshape(128, 256),
            plane[after & 3, after >> 2, 0:2].reshape(32, 256),
        ]
        pieces[0] = jnp.where(owner > 0, pieces[0], jnp.zeros_like(pieces[0]))
        pieces[2] = jnp.where(owner < last, pieces[2], jnp.zeros_like(pieces[2]))
        w = jnp.concatenate(pieces, axis=0)
        along = x_ref[cols[n]]
        none = jnp.zeros_like(along)
        upper = jnp.concatenate([along, none], axis=0)
        paired = jnp.concatenate([upper, jnp.concatenate([none, along], axis=0)], axis=1)
        t_buf[:, :256] = jnp.dot(w[:, :128], paired, preferred_element_type=f32).astype(bf16)
        t_buf[:, 256:] = jnp.dot(w[:, 128:], upper, preferred_element_type=f32).astype(bf16)

    def results(n):
        return [
            pltpu.make_async_copy(out_buf.at[f], ref.at[n], out_sem.at[f])
            for f, ref in enumerate((oimg_ref, omom_ref))
        ]

    def before_near():
        landed(first, near)
        start(first, knight)
        landed(first, diagonal)
        start(second, diagonal)

    def before_diagonal():
        landed(second, diagonal)
        landed(first, knight)
        start(second, knight)

    def before_knight():
        landed(first, [15])
        landed(second, knight)
        start(second, [15])

    hooks = {
        1: before_near,
        3: lambda: start(first, [15]),
        5: before_diagonal,
        7: lambda: start(first, [13, 14]),
        9: before_knight,
        13: lambda: landed(first, [13, 14]),
        15: lambda: landed(second, [15]),
    }

    def work(n, c):
        for at, hook in hooks.items():
            pl.when(n == at)(hook)

        @pl.when(n == 0)
        def _():
            in_buf[...] = stage[0]
            window(n)

        @pl.when(n > 0)
        def _():
            fetch = pltpu.make_async_copy(arr_ref.at[n], in_buf, in_sem)
            fetch.start()
            window(n)
            for done in results(n - 1):
                done.wait()
            fetch.wait()

        brick(n, in_buf, a2_ref, a1_ref, a0_ref, t_buf, l_ref, dz_ref, dx_ref, out_buf, s1, s2, s3, s4, s5)
        for out in results(n):
            out.start()
        return c

    lax.fori_loop(0, COUNT, work, 0)
    for done in results(COUNT - 1):
        done.wait()
    for copies in (first, second):
        for c in copies.values():
            c.wait_send()


def place_kernel(info, img_ref, mom_ref, oimg_ref, omom_ref):
    live = info[COUNT + pl.program_id(0)]

    @pl.when(live != 0)
    def _():
        oimg_ref[...] = img_ref[...]
        omom_ref[...] = mom_ref[...]

    @pl.when(live == 0)
    def _():
        oimg_ref[...] = jnp.zeros_like(oimg_ref)
        omom_ref[...] = jnp.zeros_like(omom_ref)


def place(info, image, moment):
    block = (1,) + image.shape[1:]
    return pl.pallas_call(
        place_kernel,
        grid_spec=pltpu.PrefetchScalarGridSpec(
            num_scalar_prefetch=1,
            grid=(COUNT,),
            in_specs=[pl.BlockSpec(block, lambda j, info: (info[j], 0, 0))] * 2,
            out_specs=[pl.BlockSpec(block, lambda j, info: (j, 0, 0))] * 2,
        ),
        out_shape=[jax.ShapeDtypeStruct(image.shape, image.dtype)] * 2,
        compiler_params=pltpu.CompilerParams(vmem_limit_bytes=60 * 1024 * 1024),
        name="place",
    )(info, image, moment)


def local(source, momentum, velocity, up_taps, smooth_taps, weights, slot_brick):
    me = lax.axis_index("grp")
    my_z, my_x = me // rows_x, me % rows_x
    off_z = jnp.array([o[0] for o in ORDER], jnp.int32)
    off_x = jnp.array([o[1] for o in ORDER], jnp.int32)
    targets = ((my_z + off_z) % rows_z) * rows_x + (my_x + off_x) % rows_x
    owners = ((my_z - off_z) % rows_z) * rows_x + (my_x - off_x) % rows_x
    rows = jnp.take(slot_brick, targets, axis=0)
    picks = jnp.sum(jnp.where((rows >> 3) == me, rows & 7, 0), axis=1)

    slot_ids = jnp.take(slot_brick, me, axis=0)
    slot_range = jnp.arange(COUNT, dtype=jnp.int32)
    match = (slot_ids >> 3)[None, :] == owners[:, None]
    slot_of = jnp.sum(jnp.where(match, slot_range[None, :], 0), axis=1)
    cols = jnp.sum(jnp.where(match, slot_ids[None, :] & 7, 0), axis=1)
    block_of = jnp.sum(jnp.where(match, slot_range[:, None], 0), axis=0)
    info = jnp.concatenate([block_of, (slot_ids >= 0).astype(jnp.int32)])

    coarse = edge // 8
    flat = velocity[0].transpose(2, 1, 0, 3).reshape(coarse, coarse, 3 * edge).astype(bf16)
    flat = jnp.pad(flat, ((0, 0), (0, 0), (0, edge)))
    mid = jnp.pad(flat, ((0, 0), (2, 6), (0, 0)))
    up = jnp.pad(flat[:, coarse - 2 :], ((0, 0), (0, 14), (0, 0)))
    down = jnp.pad(flat[:, :2], ((0, 0), (10, 4), (0, 0)))

    matrix = shape_matrix(up_taps, smooth_taps, coarse + 4)
    column_ids = np.arange(8)[:, None, None]
    x_ids = np.arange(edge)[None, :, None]
    places = x_ids == coarse * column_ids - 2 + np.arange(coarse + 4)[None, None, :]
    doubled = jnp.concatenate([matrix, matrix], axis=0).astype(bf16)
    along_x = jnp.einsum(
        "gkj,cj->gkc", places.astype(bf16), doubled, preferred_element_type=f32
    ).astype(bf16)
    padded = jnp.pad(matrix, ((0, 0), (0, 4)))
    left_v = (matrix[:8, :5][:, None, :, None] * padded[None, :, None, :]).reshape(8 * edge, 80)
    left_v = left_v.astype(bf16)

    mats = jnp.take(weights, slot_of, axis=0)
    a0, a1, a2 = (mats[:, :, d * edge : (d + 1) * edge] for d in range(3))
    a2 = jnp.concatenate([a2, a2], axis=1).transpose(0, 2, 1)
    difference = difference_matrix()
    diff_z = jnp.asarray(difference, bf16)
    diff_x = jnp.asarray(np.kron(np.eye(4, dtype=np.float32), difference.T), bf16)

    block = source.shape[1:]
    result = jax.ShapeDtypeStruct((COUNT,) + block, bf16)
    moved = jax.ShapeDtypeStruct((COUNT, 2) + block, bf16)
    cells = edge * edge
    dma = pltpu.SemaphoreType.DMA
    smem, vmem, hbm = (pl.BlockSpec(memory_space=m) for m in (pltpu.SMEM, pltpu.VMEM, pl.ANY))
    image, moment, _, _ = pl.pallas_call(
        shoot_kernel,
        out_shape=[result, result, moved, moved],
        in_specs=[smem] * 3 + [vmem] * 12,
        out_specs=[hbm] * 4,
        scratch_shapes=[
            pltpu.VMEM((COUNT, 2) + block, bf16),
            pltpu.VMEM((2,) + block, bf16),
            pltpu.VMEM((2,) + block, bf16),
            pltpu.VMEM((rows_x, rows_z) + mid.shape, bf16),
            pltpu.VMEM((2,) + mid.shape, bf16),
            pltpu.VMEM((192, 384), bf16),
            pltpu.VMEM((edge * PITCH, 128), f32),
            pltpu.VMEM((edge * PITCH, 128), f32),
            pltpu.VMEM((cells, 128), f32),
            pltpu.VMEM((cells, 128), f32),
            pltpu.VMEM((cells + 128, 128), f32),
            dma((COUNT, 2)),
            dma((COUNT, 2)),
            dma((COUNT, 2)),
            dma((COUNT, 2)),
            dma((8,)),
            dma((8,)),
            dma,
            dma((2,)),
        ],
        compiler_params=pltpu.CompilerParams(
            collective_id=0, has_side_effects=True, vmem_limit_bytes=58 * 1024 * 1024
        ),
        name="shoot",
    )(picks, cols, owners, source, momentum, mid, up, down, along_x, a2, a1, a0, left_v, diff_z, diff_x)
    return tuple(place(info, image, moment))


def solution(mesh):
    placed = (
        P(("slab", "grp"), None, None),
        P(("slab", "grp"), None, None),
        P(None, None, "slab", "grp", None),
        P(),
        P(),
        P(("slab", "grp"), None, None),
        P("slab", None),
    )
    return jax.shard_map(
        local,
        mesh=mesh,
        in_specs=placed,
        out_specs=(P(("slab", "grp"), None, None), P(("slab", "grp"), None, None)),
        check_vma=False,
    )
```

```python
import functools

import jax
import jax.numpy as jnp
import numpy as np
from jax import lax
from jax.experimental import pallas as pl
from jax.experimental.pallas import tpu as pltpu
from jax.sharding import PartitionSpec as P

step_time = 0.5
highest = lax.Precision.HIGHEST
edge = 64
rows_z = 4
rows_x = 4
f32 = jnp.float32
bf16 = jnp.bfloat16

PITCH = 72
UNROLL = 8
MESH = pl.DeviceIdType.MESH

NEAR = ((0, 1), (0, 3), (1, 0), (3, 0))
DIAGONAL = ((1, 1), (1, 3), (3, 1), (3, 3))
KNIGHT = ((2, 1), (2, 3), (1, 2), (3, 2))
FAR = ((2, 2), (0, 2), (2, 0))
ORDER = ((0, 0),) + NEAR + DIAGONAL + KNIGHT + FAR
COUNT = len(ORDER)


def shape_matrix(up_taps, smooth_taps, window_len):
    row_ids = jnp.arange(edge, dtype=jnp.int32)[:, None, None]
    col_ids = jnp.arange(window_len, dtype=jnp.int32)[None, :, None]
    tap_ids = jnp.arange(17, dtype=jnp.int32)[None, None, :]
    up_ids = jnp.arange(16, dtype=jnp.int32)[None, None, None, :]
    tap_index = row_ids + tap_ids - 8 * col_ids + 12
    chosen = (tap_index[..., None] == up_ids).astype(f32)
    return jnp.sum(chosen * up_taps * smooth_taps[:, None], axis=(2, 3))


def difference_matrix():
    difference = np.zeros((edge, edge), np.float32)
    for r in range(edge):
        lower, upper = max(r - 1, 0), min(r + 1, edge - 1)
        difference[r, upper] += 1.0 / (upper - lower)
        difference[r, lower] -= 1.0 / (upper - lower)
    return difference


def brick(n, in_ref, a2_ref, a1_ref, a0_ref, t_ref, l_ref, dz_ref, dx_ref, out_ref, s1, s2, s3, s4, s5):
    left = lax.broadcasted_iota(jnp.int32, (1, 128), 1) < edge

    a2 = a2_ref[n]
    none = jnp.zeros_like(a2)
    halves = [jnp.where(left, a2, none), jnp.where(left, none, a2)]
    w2 = jnp.concatenate(
        [jnp.concatenate(p, axis=1) for half in halves for p in ((half, none), (none, half))], axis=0
    )

    def x_pass(h, c):
        pieces = []
        for k in range(4):
            at = pl.ds(pl.multiple_of(h * 512 + k * 128, 128), 128)
            pieces.append(jnp.concatenate([in_ref[0, :, at], in_ref[1, :, at]], axis=1))
        res = jnp.dot(jnp.concatenate(pieces, axis=0), w2, preferred_element_type=f32)
        for k in range(4):
            for p in range(2):
                row = pl.multiple_of((h * 8 + 2 * k + p) * PITCH, 8)
                s1[pl.ds(row, 64), :] = res[k * 64 : (k + 1) * 64, p * 128 : (p + 1) * 128]
        return c

    lax.fori_loop(0, 8, x_pass, 0, unroll=UNROLL)

    def y_pass(h, c):
        cols = [s1[pl.ds(h * 8 + i, 64, stride=PITCH), :].astype(bf16) for i in range(8)]
        res = jnp.dot(a1_ref[n], jnp.concatenate(cols, axis=1), preferred_element_type=f32)
        for i in range(8):
            row = pl.multiple_of((h * 8 + i) * PITCH, 8)
            s2[pl.ds(row, 64), :] = res[:, i * 128 : (i + 1) * 128]
        return c

    lax.fori_loop(0, 8, y_pass, 0, unroll=UNROLL)

    def to_rows(x):
        return jnp.concatenate([x[:, i * 128 : (i + 1) * 128] for i in range(8)], axis=0)

    def to_cols(x):
        return jnp.concatenate([x[i * 64 : (i + 1) * 64] for i in range(8)], axis=1)

    def z_pass(h, c):
        cols = [s2[pl.ds(h * 8 + i, 64, stride=PITCH), :].astype(bf16) for i in range(8)]
        j = to_rows(
            jnp.dot(a0_ref[n], jnp.concatenate(cols, axis=1), preferred_element_type=f32)
        )
        at = pl.ds(pl.multiple_of(h * 16, 16), 80)
        v = jnp.dot(l_ref[...], t_ref[at, :], preferred_element_type=f32)
        vz, vy, vx = v[:, :128], v[:, 128:256], v[:, 256:]
        carry_z = jnp.where(left, j, vz * j).astype(bf16)
        carry_y = jnp.where(left, j, vy * j).astype(bf16)
        carry_x = jnp.where(left, j, vx * j).astype(bf16)
        gz = to_rows(jnp.dot(dz_ref[...], to_cols(carry_z), preferred_element_type=f32))
        pairs = jnp.concatenate(
            [
                jnp.concatenate(
                    [carry_x[(2 * k) * 64 : (2 * k + 1) * 64], carry_x[(2 * k + 1) * 64 : (2 * k + 2) * 64]],
                    axis=1,
                )
                for k in range(4)
            ],
            axis=0,
        )
        gp = jnp.dot(pairs, dx_ref[...], preferred_element_type=f32)
        gx = jnp.concatenate(
            [gp[k * 64 : (k + 1) * 64, p * 128 : (p + 1) * 128] for k in range(4) for p in range(2)],
            axis=0,
        )
        upd = jnp.where(left, vz, 1.0) * gz + jnp.where(left, vx, 1.0) * gx
        row = pl.multiple_of(h * 512, 512)
        s3[pl.ds(row, 512), :] = j - step_time * upd
        s4[pl.ds(row, 512), :] = (0.5 * step_time) * jnp.where(left, vy, 1.0)
        s5[pl.ds(row + 64, 512), :] = carry_y.astype(f32)
        return c

    lax.fori_loop(0, 8, z_pass, 0, unroll=UNROLL)
    s5[0:64, :] = 2.0 * s5[64:128, :] - s5[128:192, :]
    s5[65 * 64 : 66 * 64, :] = 2.0 * s5[64 * 64 : 65 * 64, :] - s5[63 * 64 : 64 * 64, :]

    def finish(h, c):
        for k in range(4):
            o = []
            for p in range(2):
                row = pl.multiple_of(h * 512 + (2 * k + p) * 64, 64)
                diff = s5[pl.ds(row + 128, 64), :] - s5[pl.ds(row, 64), :]
                o.append(s3[pl.ds(row, 64), :] - s4[pl.ds(row, 64), :] * diff)
            at = pl.ds(pl.multiple_of(h * 512 + k * 128, 128), 128)
            img = jnp.where(left, o[0], pltpu.roll(o[1], 64, 1))
            mom = jnp.where(left, pltpu.roll(o[0], 64, 1), o[1])
            out_ref[0, :, at] = img.astype(bf16)
            out_ref[1, :, at] = mom.astype(bf16)
        return c

    lax.fori_loop(0, 8, finish, 0, unroll=UNROLL)


def shoot_kernel(
    picks, cols, owners, src_ref, mom_ref, mid_ref, edge_ref, x_ref, a2_ref, a1_ref, a0_ref,
    l_ref, dz_ref, dx_ref,
    oimg_ref, omom_ref, arr_ref, inter_ref,
    stage, in_buf, out_buf, plane, halo, t_buf, s1, s2, s3, s4, s5,
    send1, recv1, send2, recv2, vsend, vrecv, in_sem, out_sem,
):
    grp, slab = lax.axis_index("grp"), lax.axis_index("slab")
    my_z, my_x = grp // rows_x, grp % rows_x
    slabs = lax.axis_size("slab")

    def at_offset(dz, dx):
        return {"slab": slab, "grp": lax.rem(my_z + dz, rows_z) * rows_x + lax.rem(my_x + dx, rows_x)}

    def at_slab(step):
        return {"slab": lax.rem(slab + step + slabs, slabs), "grp": grp}

    barrier = pltpu.get_barrier_semaphore()
    peers = [at_offset(d, 0) for d in (1, 2, 3)] + [at_offset(0, d) for d in (1, 2, 3)]
    peers += [at_slab(1), at_slab(-1)]
    for peer in peers:
        pl.semaphore_signal(barrier, inc=1, device_id=peer, device_id_type=MESH)
    pl.semaphore_wait(barrier, len(peers))

    def remote(src, dst, send, recv, device):
        return pltpu.make_async_remote_copy(
            src_ref=src, dst_ref=dst, send_sem=send, recv_sem=recv, device_id=device, device_id_type=MESH
        )

    halos = [
        remote(edge_ref, halo.at[0], vsend.at[0], vrecv.at[0], at_slab(1)),
        remote(edge_ref, halo.at[1], vsend.at[1], vrecv.at[1], at_slab(-1)),
    ]
    for c in halos:
        c.start()

    first, second = {}, {}
    for n, (dz, dx) in enumerate(ORDER):
        if n == 0:
            continue
        both = dz != 0 and dx != 0
        for f in range(2):
            leg1 = at_offset(dz, 0) if (f == 0) == (dz != 0) or dx == 0 else at_offset(0, dx)
            if not both:
                leg1 = at_offset(dz, dx)
            into = inter_ref.at[n, f] if both else arr_ref.at[n, f]
            first[n, f] = remote(stage.at[n, f], into, send1.at[n, f], recv1.at[n, f], leg1)
            if both:
                leg2 = at_offset(0, dx) if f == 0 else at_offset(dz, 0)
                second[n, f] = remote(
                    inter_ref.at[n, f], arr_ref.at[n, f], send2.at[n, f], recv2.at[n, f], leg2
                )

    def put(n, c):
        stage[n, 0] = src_ref[picks[n]]
        stage[n, 1] = mom_ref[picks[n]]
        return c

    def start(copies, ns):
        for n in ns:
            for f in range(2):
                copies[n, f].start()

    def landed(copies, ns):
        for n in ns:
            for f in range(2):
                copies[n, f].wait_recv()

    near, diagonal, knight = range(1, 5), range(5, 9), range(9, 13)
    for group in (near, diagonal, knight):
        lax.fori_loop(group[0], group[-1] + 1, put, 0)
        start(first, group)

    for c in halos:
        c.wait()
    piece = mid_ref[...]
    layer = lax.broadcasted_iota(jnp.int32, piece.shape, 1)
    below = (layer < 2) & (slab > 0)
    above = (layer >= 10) & (layer < 12) & (slab < slabs - 1)
    plane[my_x, my_z] = jnp.where(below, halo[0], jnp.where(above, halo[1], piece))
    lower, upper = pl.ds(0, 4), pl.ds(4, 4)
    mine_lower, mine_upper = plane.at[my_x, my_z, lower], plane.at[my_x, my_z, upper]
    leg1 = [remote(mine_lower, mine_lower, vsend.at[1 + d], vrecv.at[1 + d], at_offset(d, 0)) for d in (1, 2, 3)]
    leg1 += [remote(mine_upper, mine_upper, vsend.at[4 + d], vrecv.at[4 + d], at_offset(0, d)) for d in (1, 2, 3)]
    for c in leg1:
        c.start()
    lax.fori_loop(13, 16, put, 0)
    for c in leg1:
        c.wait()
    row_lower, row_upper = plane.at[my_x, :, lower], plane.at[:, my_z, upper]
    leg2 = [remote(row_lower, row_lower, vsend.at[7 + d], vrecv.at[7 + d], at_offset(0, d)) for d in (1, 2, 3)]
    leg2 += [remote(row_upper, row_upper, vsend.at[10 + d], vrecv.at[10 + d], at_offset(d, 0)) for d in (1, 2, 3)]
    for c in leg2:
        c.start()
    lax.fori_loop(0, 1, put, 0)
    for c in leg2:
        c.wait()

    def window(n):
        owner, last = owners[n], rows_z * rows_x - 1
        before, after = jnp.maximum(owner - 1, 0), jnp.minimum(owner + 1, last)
        pieces = [
            plane[before & 3, before >> 2, 6:8].reshape(32, 256),
            plane[owner & 3, owner >> 2].reshape(128, 256),
            plane[after & 3, after >> 2, 0:2].reshape(32, 256),
        ]
        pieces[0] = jnp.where(owner > 0, pieces[0], jnp.zeros_like(pieces[0]))
        pieces[2] = jnp.where(owner < last, pieces[2], jnp.zeros_like(pieces[2]))
        w = jnp.concatenate(pieces, axis=0)
        along = x_ref[cols[n]]
        none = jnp.zeros_like(along)
        upper = jnp.concatenate([along, none], axis=0)
        paired = jnp.concatenate([upper, jnp.concatenate([none, along], axis=0)], axis=1)
        t_buf[:, :256] = jnp.dot(w[:, :128], paired, preferred_element_type=f32).astype(bf16)
        t_buf[:, 256:] = jnp.dot(w[:, 128:], upper, preferred_element_type=f32).astype(bf16)

    def results(n):
        return [
            pltpu.make_async_copy(out_buf.at[f], ref.at[n], out_sem.at[f])
            for f, ref in enumerate((oimg_ref, omom_ref))
        ]

    def before_near():
        landed(first, diagonal)
        start(second, diagonal)
        start(first, [13])
        landed(first, near)

    def before_diagonal():
        landed(first, knight)
        start(second, knight)
        landed(first, [13])
        start(second, [13])
        landed(second, diagonal)

    def before_knight():
        landed(second, knight)
        start(first, [14, 15])

    hooks = {
        1: before_near,
        5: before_diagonal,
        9: before_knight,
        13: lambda: landed(second, [13]),
        14: lambda: landed(first, [14, 15]),
    }

    def fetch(n):
        return pltpu.make_async_copy(arr_ref.at[n], in_buf.at[n % 2], in_sem.at[n % 2])

    def work(n, c):
        for at, hook in hooks.items():
            pl.when(n == at)(hook)

        opens = (n == 1) | (n == 5) | (n == 9) | (n == 13) | (n == 14)
        ends = (n == 0) | (n == 4) | (n == 8) | (n == 12) | (n == 13) | (n == 15)

        @pl.when(n == 0)
        def _():
            in_buf[0] = stage[0]

        @pl.when(opens)
        def _():
            fetch(n).start()

        window(n)

        @pl.when(n > 0)
        def _():
            for done in results(n - 1):
                done.wait()
            fetch(n).wait()

        @pl.when(jnp.logical_not(ends))
        def _():
            fetch(n + 1).start()

        brick(
            n, in_buf.at[n % 2], a2_ref, a1_ref, a0_ref, t_buf, l_ref, dz_ref, dx_ref, out_buf, s1, s2, s3, s4, s5
        )
        for out in results(n):
            out.start()
        return c

    lax.fori_loop(0, COUNT, work, 0)
    for done in results(COUNT - 1):
        done.wait()
    for copies in (first, second):
        for c in copies.values():
            c.wait_send()


def place_kernel(info, img_ref, mom_ref, oimg_ref, omom_ref, held, zeros, in_sem, out_sem):
    fields = ((img_ref, oimg_ref), (mom_ref, omom_ref))

    def read(j, f):
        return pltpu.make_async_copy(fields[f][0].at[info[j]], held.at[j, f], in_sem.at[j, f])

    def write(j, f, source):
        return pltpu.make_async_copy(source, fields[f][1].at[j], out_sem.at[j, f])

    def begin(j, c):
        @pl.when(info[COUNT + j] != 0)
        def _():
            read(j, 0).start()
            read(j, 1).start()

        return c

    lax.fori_loop(0, COUNT, begin, 0)
    zeros[...] = jnp.zeros_like(zeros)

    def move(j, c):
        @pl.when(info[COUNT + j] != 0)
        def _():
            for f in range(2):
                read(j, f).wait()
                write(j, f, held.at[j, f]).start()

        @pl.when(info[COUNT + j] == 0)
        def _():
            for f in range(2):
                write(j, f, zeros).start()

        return c

    lax.fori_loop(0, COUNT, move, 0)

    def end(j, c):
        for f in range(2):
            write(j, f, zeros).wait()
        return c

    lax.fori_loop(0, COUNT, end, 0)


def place(info, image, moment):
    block = image.shape[1:]
    hbm = pl.BlockSpec(memory_space=pl.ANY)
    return pl.pallas_call(
        place_kernel,
        grid_spec=pltpu.PrefetchScalarGridSpec(
            num_scalar_prefetch=1,
            grid=(1,),
            in_specs=[hbm] * 2,
            out_specs=[hbm] * 2,
            scratch_shapes=[
                pltpu.VMEM((COUNT, 2) + block, bf16),
                pltpu.VMEM(block, bf16),
                pltpu.SemaphoreType.DMA((COUNT, 2)),
                pltpu.SemaphoreType.DMA((COUNT, 2)),
            ],
        ),
        out_shape=[jax.ShapeDtypeStruct(image.shape, image.dtype)] * 2,
        compiler_params=pltpu.CompilerParams(vmem_limit_bytes=60 * 1024 * 1024),
        name="place",
    )(info, image, moment)


def local(source, momentum, velocity, up_taps, smooth_taps, weights, slot_brick):
    me = lax.axis_index("grp")
    my_z, my_x = me // rows_x, me % rows_x
    off_z = jnp.array([o[0] for o in ORDER], jnp.int32)
    off_x = jnp.array([o[1] for o in ORDER], jnp.int32)
    targets = ((my_z + off_z) % rows_z) * rows_x + (my_x + off_x) % rows_x
    owners = ((my_z - off_z) % rows_z) * rows_x + (my_x - off_x) % rows_x
    rows = jnp.take(slot_brick, targets, axis=0)
    picks = jnp.sum(jnp.where((rows >> 3) == me, rows & 7, 0), axis=1)

    slot_ids = jnp.take(slot_brick, me, axis=0)
    slot_range = jnp.arange(COUNT, dtype=jnp.int32)
    match = (slot_ids >> 3)[None, :] == owners[:, None]
    slot_of = jnp.sum(jnp.where(match, slot_range[None, :], 0), axis=1)
    cols = jnp.sum(jnp.where(match, slot_ids[None, :] & 7, 0), axis=1)
    block_of = jnp.sum(jnp.where(match, slot_range[:, None], 0), axis=0)
    info = jnp.concatenate([block_of, (slot_ids >= 0).astype(jnp.int32)])

    coarse = edge // 8
    flat = velocity[0].transpose(2, 1, 0, 3).reshape(coarse, coarse, 3 * edge).astype(bf16)
    flat = jnp.pad(flat, ((0, 0), (0, 0), (0, edge)))
    mid = jnp.pad(flat, ((0, 0), (2, 6), (0, 0)))
    edges = jnp.roll(mid, 8, axis=1)

    matrix = shape_matrix(up_taps, smooth_taps, coarse + 4)
    column_ids = np.arange(8)[:, None, None]
    x_ids = np.arange(edge)[None, :, None]
    places = x_ids == coarse * column_ids - 2 + np.arange(coarse + 4)[None, None, :]
    doubled = jnp.concatenate([matrix, matrix], axis=0).astype(bf16)
    along_x = jnp.einsum(
        "gkj,cj->gkc", places.astype(bf16), doubled, preferred_element_type=f32
    ).astype(bf16)
    padded = jnp.pad(matrix, ((0, 0), (0, 4)))
    left_v = (matrix[:8, :5][:, None, :, None] * padded[None, :, None, :]).reshape(8 * edge, 80)
    left_v = left_v.astype(bf16)

    mats = jnp.take(weights, slot_of, axis=0)
    a0, a1, a2 = (mats[:, :, d * edge : (d + 1) * edge] for d in range(3))
    a2 = jnp.concatenate([a2, a2], axis=1).transpose(0, 2, 1)
    difference = difference_matrix()
    diff_z = jnp.asarray(difference, bf16)
    diff_x = jnp.asarray(np.kron(np.eye(4, dtype=np.float32), difference.T), bf16)

    block = source.shape[1:]
    result = jax.ShapeDtypeStruct((COUNT,) + block, bf16)
    moved = jax.ShapeDtypeStruct((COUNT, 2) + block, bf16)
    cells = edge * edge
    dma = pltpu.SemaphoreType.DMA
    smem, vmem, hbm = (pl.BlockSpec(memory_space=m) for m in (pltpu.SMEM, pltpu.VMEM, pl.ANY))
    image, moment, _, _ = pl.pallas_call(
        shoot_kernel,
        out_shape=[result, result, moved, moved],
        in_specs=[smem] * 3 + [vmem] * 11,
        out_specs=[hbm] * 4,
        scratch_shapes=[
            pltpu.VMEM((COUNT, 2) + block, bf16),
            pltpu.VMEM((2, 2) + block, bf16),
            pltpu.VMEM((2,) + block, bf16),
            pltpu.VMEM((rows_x, rows_z) + mid.shape, bf16),
            pltpu.VMEM((2,) + mid.shape, bf16),
            pltpu.VMEM((192, 384), bf16),
            pltpu.VMEM((edge * PITCH, 128), f32),
            pltpu.VMEM((edge * PITCH, 128), f32),
            pltpu.VMEM((cells, 128), f32),
            pltpu.VMEM((cells, 128), f32),
            pltpu.VMEM((cells + 128, 128), f32),
            dma((COUNT, 2)),
            dma((COUNT, 2)),
            dma((COUNT, 2)),
            dma((COUNT, 2)),
            dma((14,)),
            dma((14,)),
            dma((2,)),
            dma((2,)),
        ],
        compiler_params=pltpu.CompilerParams(
            collective_id=0, has_side_effects=True, vmem_limit_bytes=58 * 1024 * 1024
        ),
        name="shoot",
    )(picks, cols, owners, source, momentum, mid, edges, along_x, a2, a1, a0, left_v, diff_z, diff_x)
    return tuple(place(info, image, moment))


def solution(mesh):
    placed = (
        P(("slab", "grp"), None, None),
        P(("slab", "grp"), None, None),
        P(None, None, "slab", "grp", None),
        P(),
        P(),
        P(("slab", "grp"), None, None),
        P("slab", None),
    )
    return jax.shard_map(
        local,
        mesh=mesh,
        in_specs=placed,
        out_specs=(P(("slab", "grp"), None, None), P(("slab", "grp"), None, None)),
        check_vma=False,
    )
```

```python
import functools

import jax
import jax.numpy as jnp
import numpy as np
from jax import lax
from jax.experimental import pallas as pl
from jax.experimental.pallas import tpu as pltpu
from jax.sharding import PartitionSpec as P

step_time = 0.5
highest = lax.Precision.HIGHEST
edge = 64
rows_z = 4
rows_x = 4
f32 = jnp.float32
bf16 = jnp.bfloat16

PITCH = 72
UNROLL = 8
MESH = pl.DeviceIdType.MESH

NEAR = ((0, 1), (0, 3), (1, 0), (3, 0))
DIAGONAL = ((1, 1), (1, 3), (3, 1), (3, 3))
CORNER = ((2, 2),)
KNIGHT = ((2, 1), (1, 2), (2, 3), (3, 2))
FAR = ((0, 2), (2, 0))
ORDER = ((0, 0),) + NEAR + DIAGONAL + CORNER + KNIGHT + FAR
COUNT = len(ORDER)


def shape_matrix(up_taps, smooth_taps, window_len):
    row_ids = jnp.arange(edge, dtype=jnp.int32)[:, None, None]
    col_ids = jnp.arange(window_len, dtype=jnp.int32)[None, :, None]
    tap_ids = jnp.arange(17, dtype=jnp.int32)[None, None, :]
    up_ids = jnp.arange(16, dtype=jnp.int32)[None, None, None, :]
    tap_index = row_ids + tap_ids - 8 * col_ids + 12
    chosen = (tap_index[..., None] == up_ids).astype(f32)
    return jnp.sum(chosen * up_taps * smooth_taps[:, None], axis=(2, 3))


def difference_matrix():
    difference = np.zeros((edge, edge), np.float32)
    for r in range(edge):
        lower, upper = max(r - 1, 0), min(r + 1, edge - 1)
        difference[r, upper] += 1.0 / (upper - lower)
        difference[r, lower] -= 1.0 / (upper - lower)
    return difference


def brick(n, in_ref, a2_ref, a1_ref, a0_ref, t_ref, l_ref, dz_ref, dx_ref, out_ref, s1, s2, s3, s4, s5):
    left = lax.broadcasted_iota(jnp.int32, (1, 128), 1) < edge

    a2 = a2_ref[n]
    none = jnp.zeros_like(a2)
    halves = [jnp.where(left, a2, none), jnp.where(left, none, a2)]
    w2 = jnp.concatenate(
        [jnp.concatenate(p, axis=1) for half in halves for p in ((half, none), (none, half))], axis=0
    )

    def x_pass(h, c):
        pieces = []
        for k in range(4):
            at = pl.ds(pl.multiple_of(h * 512 + k * 128, 128), 128)
            pieces.append(jnp.concatenate([in_ref[0, :, at], in_ref[1, :, at]], axis=1))
        res = jnp.dot(jnp.concatenate(pieces, axis=0), w2, preferred_element_type=f32)
        for k in range(4):
            for p in range(2):
                row = pl.multiple_of((h * 8 + 2 * k + p) * PITCH, 8)
                s1[pl.ds(row, 64), :] = res[k * 64 : (k + 1) * 64, p * 128 : (p + 1) * 128]
        return c

    lax.fori_loop(0, 8, x_pass, 0, unroll=UNROLL)

    def y_pass(h, c):
        cols = [s1[pl.ds(h * 8 + i, 64, stride=PITCH), :].astype(bf16) for i in range(8)]
        res = jnp.dot(a1_ref[n], jnp.concatenate(cols, axis=1), preferred_element_type=f32)
        for i in range(8):
            row = pl.multiple_of((h * 8 + i) * PITCH, 8)
            s2[pl.ds(row, 64), :] = res[:, i * 128 : (i + 1) * 128]
        return c

    lax.fori_loop(0, 8, y_pass, 0, unroll=UNROLL)

    def to_rows(x):
        return jnp.concatenate([x[:, i * 128 : (i + 1) * 128] for i in range(8)], axis=0)

    def to_cols(x):
        return jnp.concatenate([x[i * 64 : (i + 1) * 64] for i in range(8)], axis=1)

    def z_pass(h, c):
        cols = [s2[pl.ds(h * 8 + i, 64, stride=PITCH), :].astype(bf16) for i in range(8)]
        j = to_rows(
            jnp.dot(a0_ref[n], jnp.concatenate(cols, axis=1), preferred_element_type=f32)
        )
        at = pl.ds(pl.multiple_of(h * 16, 16), 80)
        v = jnp.dot(l_ref[...], t_ref[at, :], preferred_element_type=f32)
        vz, vy, vx = v[:, :128], v[:, 128:256], v[:, 256:]
        carry_z = jnp.where(left, j, vz * j).astype(bf16)
        carry_y = jnp.where(left, j, vy * j).astype(bf16)
        carry_x = jnp.where(left, j, vx * j).astype(bf16)
        gz = to_rows(jnp.dot(dz_ref[...], to_cols(carry_z), preferred_element_type=f32))
        pairs = jnp.concatenate(
            [
                jnp.concatenate(
                    [carry_x[(2 * k) * 64 : (2 * k + 1) * 64], carry_x[(2 * k + 1) * 64 : (2 * k + 2) * 64]],
                    axis=1,
                )
                for k in range(4)
            ],
            axis=0,
        )
        gp = jnp.dot(pairs, dx_ref[...], preferred_element_type=f32)
        gx = jnp.concatenate(
            [gp[k * 64 : (k + 1) * 64, p * 128 : (p + 1) * 128] for k in range(4) for p in range(2)],
            axis=0,
        )
        upd = jnp.where(left, vz, 1.0) * gz + jnp.where(left, vx, 1.0) * gx
        row = pl.multiple_of(h * 512, 512)
        s3[pl.ds(row, 512), :] = j - step_time * upd
        s4[pl.ds(row, 512), :] = (0.5 * step_time) * jnp.where(left, vy, 1.0)
        s5[pl.ds(row + 64, 512), :] = carry_y.astype(f32)
        return c

    lax.fori_loop(0, 8, z_pass, 0, unroll=UNROLL)
    s5[0:64, :] = 2.0 * s5[64:128, :] - s5[128:192, :]
    s5[65 * 64 : 66 * 64, :] = 2.0 * s5[64 * 64 : 65 * 64, :] - s5[63 * 64 : 64 * 64, :]

    def finish(h, c):
        for k in range(4):
            o = []
            for p in range(2):
                row = pl.multiple_of(h * 512 + (2 * k + p) * 64, 64)
                diff = s5[pl.ds(row + 128, 64), :] - s5[pl.ds(row, 64), :]
                o.append(s3[pl.ds(row, 64), :] - s4[pl.ds(row, 64), :] * diff)
            at = pl.ds(pl.multiple_of(h * 512 + k * 128, 128), 128)
            img = jnp.where(left, o[0], pltpu.roll(o[1], 64, 1))
            mom = jnp.where(left, pltpu.roll(o[0], 64, 1), o[1])
            out_ref[0, :, at] = img.astype(bf16)
            out_ref[1, :, at] = mom.astype(bf16)
        return c

    lax.fori_loop(0, 8, finish, 0, unroll=UNROLL)


def shoot_kernel(
    picks, cols, owners, src_ref, mom_ref, mid_ref, edge_ref, x_ref, a2_ref, a1_ref, a0_ref,
    l_ref, dz_ref, dx_ref,
    oimg_ref, omom_ref, arr_ref, inter_ref,
    stage, in_buf, out_buf, plane, halo, t_buf, s1, s2, s3, s4, s5,
    send1, recv1, send2, recv2, vsend, vrecv, in_sem, out_sem,
):
    grp, slab = lax.axis_index("grp"), lax.axis_index("slab")
    my_z, my_x = grp // rows_x, grp % rows_x
    slabs = lax.axis_size("slab")

    def at_offset(dz, dx):
        return {"slab": slab, "grp": lax.rem(my_z + dz, rows_z) * rows_x + lax.rem(my_x + dx, rows_x)}

    def at_slab(step):
        return {"slab": lax.rem(slab + step + slabs, slabs), "grp": grp}

    barrier = pltpu.get_barrier_semaphore()
    peers = [at_offset(d, 0) for d in (1, 2, 3)] + [at_offset(0, d) for d in (1, 2, 3)]
    peers += [at_slab(1), at_slab(-1)]
    for peer in peers:
        pl.semaphore_signal(barrier, inc=1, device_id=peer, device_id_type=MESH)
    pl.semaphore_wait(barrier, len(peers))

    def remote(src, dst, send, recv, device):
        return pltpu.make_async_remote_copy(
            src_ref=src, dst_ref=dst, send_sem=send, recv_sem=recv, device_id=device, device_id_type=MESH
        )

    halos = [
        remote(edge_ref, halo.at[0], vsend.at[0], vrecv.at[0], at_slab(1)),
        remote(edge_ref, halo.at[1], vsend.at[1], vrecv.at[1], at_slab(-1)),
    ]
    for c in halos:
        c.start()

    first, second = {}, {}
    for n, (dz, dx) in enumerate(ORDER):
        if n == 0:
            continue
        both = dz != 0 and dx != 0
        for f in range(2):
            leg1 = at_offset(dz, 0) if (f == 0) == (dz != 0) or dx == 0 else at_offset(0, dx)
            if not both:
                leg1 = at_offset(dz, dx)
            into = inter_ref.at[n, f] if both else arr_ref.at[n, f]
            first[n, f] = remote(stage.at[n, f], into, send1.at[n, f], recv1.at[n, f], leg1)
            if both:
                leg2 = at_offset(0, dx) if f == 0 else at_offset(dz, 0)
                second[n, f] = remote(
                    inter_ref.at[n, f], arr_ref.at[n, f], send2.at[n, f], recv2.at[n, f], leg2
                )

    def put(n, c):
        stage[n, 0] = src_ref[picks[n]]
        stage[n, 1] = mom_ref[picks[n]]
        return c

    def start(copies, ns):
        for n in ns:
            for f in range(2):
                copies[n, f].start()

    def landed(copies, ns):
        for n in ns:
            for f in range(2):
                copies[n, f].wait_recv()

    near, diagonal, corner, knight = range(1, 5), range(5, 9), [9], range(10, 14)
    for group in (near, diagonal, knight):
        lax.fori_loop(group[0], group[-1] + 1, put, 0)
        start(first, group)

    for c in halos:
        c.wait()
    piece = mid_ref[...]
    layer = lax.broadcasted_iota(jnp.int32, piece.shape, 1)
    below = (layer < 2) & (slab > 0)
    above = (layer >= 10) & (layer < 12) & (slab < slabs - 1)
    plane[my_x, my_z] = jnp.where(below, halo[0], jnp.where(above, halo[1], piece))
    lower, upper = pl.ds(0, 4), pl.ds(4, 4)
    mine_lower, mine_upper = plane.at[my_x, my_z, lower], plane.at[my_x, my_z, upper]
    leg1 = [remote(mine_lower, mine_lower, vsend.at[1 + d], vrecv.at[1 + d], at_offset(d, 0)) for d in (1, 2, 3)]
    leg1 += [remote(mine_upper, mine_upper, vsend.at[4 + d], vrecv.at[4 + d], at_offset(0, d)) for d in (1, 2, 3)]
    for c in leg1:
        c.start()
    lax.fori_loop(9, 10, put, 0)
    lax.fori_loop(14, 16, put, 0)
    for c in leg1:
        c.wait()
    row_lower, row_upper = plane.at[my_x, :, lower], plane.at[:, my_z, upper]
    leg2 = [remote(row_lower, row_lower, vsend.at[7 + d], vrecv.at[7 + d], at_offset(0, d)) for d in (1, 2, 3)]
    leg2 += [remote(row_upper, row_upper, vsend.at[10 + d], vrecv.at[10 + d], at_offset(d, 0)) for d in (1, 2, 3)]
    for c in leg2:
        c.start()
    lax.fori_loop(0, 1, put, 0)
    for c in leg2:
        c.wait()

    def window(n):
        owner, last = owners[n], rows_z * rows_x - 1
        before, after = jnp.maximum(owner - 1, 0), jnp.minimum(owner + 1, last)
        pieces = [
            plane[before & 3, before >> 2, 6:8].reshape(32, 256),
            plane[owner & 3, owner >> 2].reshape(128, 256),
            plane[after & 3, after >> 2, 0:2].reshape(32, 256),
        ]
        pieces[0] = jnp.where(owner > 0, pieces[0], jnp.zeros_like(pieces[0]))
        pieces[2] = jnp.where(owner < last, pieces[2], jnp.zeros_like(pieces[2]))
        w = jnp.concatenate(pieces, axis=0)
        along = x_ref[cols[n]]
        none = jnp.zeros_like(along)
        upper = jnp.concatenate([along, none], axis=0)
        paired = jnp.concatenate([upper, jnp.concatenate([none, along], axis=0)], axis=1)
        t_buf[:, :256] = jnp.dot(w[:, :128], paired, preferred_element_type=f32).astype(bf16)
        t_buf[:, 256:] = jnp.dot(w[:, 128:], upper, preferred_element_type=f32).astype(bf16)

    def results(n):
        return [
            pltpu.make_async_copy(out_buf.at[f], ref.at[n], out_sem.at[f])
            for f, ref in enumerate((oimg_ref, omom_ref))
        ]

    def before_near():
        landed(first, diagonal)
        start(second, diagonal)
        start(first, corner)
        landed(first, near)

    def before_diagonal():
        landed(first, knight)
        start(second, knight)
        landed(first, corner)
        start(second, corner)
        landed(second, diagonal)

    def before_knight():
        landed(second, knight[:2])
        start(first, [14, 15])

    hooks = {
        1: before_near,
        5: before_diagonal,
        9: lambda: landed(second, corner),
        10: before_knight,
        12: lambda: landed(second, knight[2:]),
        14: lambda: landed(first, [14]),
        15: lambda: landed(first, [15]),
    }

    def fetch(n):
        return pltpu.make_async_copy(arr_ref.at[n], in_buf.at[n % 2], in_sem.at[n % 2])

    def work(n, c):
        for at, hook in hooks.items():
            pl.when(n == at)(hook)

        opens, ends = n < 0, n == COUNT - 1
        for at in (1, 5, 9, 10, 12, 14, 15):
            opens = opens | (n == at)
            ends = ends | (n == at - 1)

        @pl.when(n == 0)
        def _():
            in_buf[0] = stage[0]

        @pl.when(opens)
        def _():
            fetch(n).start()

        window(n)

        @pl.when(n > 0)
        def _():
            for done in results(n - 1):
                done.wait()
            fetch(n).wait()

        @pl.when(jnp.logical_not(ends))
        def _():
            fetch(n + 1).start()

        brick(
            n, in_buf.at[n % 2], a2_ref, a1_ref, a0_ref, t_buf, l_ref, dz_ref, dx_ref, out_buf, s1, s2, s3, s4, s5
        )
        for out in results(n):
            out.start()
        return c

    lax.fori_loop(0, COUNT, work, 0)
    for done in results(COUNT - 1):
        done.wait()
    for copies in (first, second):
        for c in copies.values():
            c.wait_send()


def place_kernel(info, img_ref, mom_ref, oimg_ref, omom_ref, held, zeros, in_sem, out_sem):
    fields = ((img_ref, oimg_ref), (mom_ref, omom_ref))

    def read(j, f):
        return pltpu.make_async_copy(fields[f][0].at[info[j]], held.at[j, f], in_sem.at[j, f])

    def write(j, f, source):
        return pltpu.make_async_copy(source, fields[f][1].at[j], out_sem.at[j, f])

    def begin(j, c):
        @pl.when(info[COUNT + j] != 0)
        def _():
            read(j, 0).start()
            read(j, 1).start()

        return c

    lax.fori_loop(0, COUNT, begin, 0)
    zeros[...] = jnp.zeros_like(zeros)

    def move(j, c):
        @pl.when(info[COUNT + j] != 0)
        def _():
            for f in range(2):
                read(j, f).wait()
                write(j, f, held.at[j, f]).start()

        @pl.when(info[COUNT + j] == 0)
        def _():
            for f in range(2):
                write(j, f, zeros).start()

        return c

    lax.fori_loop(0, COUNT, move, 0)

    def end(j, c):
        for f in range(2):
            write(j, f, zeros).wait()
        return c

    lax.fori_loop(0, COUNT, end, 0)


def place(info, image, moment):
    block = image.shape[1:]
    hbm = pl.BlockSpec(memory_space=pl.ANY)
    return pl.pallas_call(
        place_kernel,
        grid_spec=pltpu.PrefetchScalarGridSpec(
            num_scalar_prefetch=1,
            grid=(1,),
            in_specs=[hbm] * 2,
            out_specs=[hbm] * 2,
            scratch_shapes=[
                pltpu.VMEM((COUNT, 2) + block, bf16),
                pltpu.VMEM(block, bf16),
                pltpu.SemaphoreType.DMA((COUNT, 2)),
                pltpu.SemaphoreType.DMA((COUNT, 2)),
            ],
        ),
        out_shape=[jax.ShapeDtypeStruct(image.shape, image.dtype)] * 2,
        compiler_params=pltpu.CompilerParams(vmem_limit_bytes=60 * 1024 * 1024),
        name="place",
    )(info, image, moment)


def local(source, momentum, velocity, up_taps, smooth_taps, weights, slot_brick):
    me = lax.axis_index("grp")
    my_z, my_x = me // rows_x, me % rows_x
    off_z = jnp.array([o[0] for o in ORDER], jnp.int32)
    off_x = jnp.array([o[1] for o in ORDER], jnp.int32)
    targets = ((my_z + off_z) % rows_z) * rows_x + (my_x + off_x) % rows_x
    owners = ((my_z - off_z) % rows_z) * rows_x + (my_x - off_x) % rows_x
    rows = jnp.take(slot_brick, targets, axis=0)
    picks = jnp.sum(jnp.where((rows >> 3) == me, rows & 7, 0), axis=1)

    slot_ids = jnp.take(slot_brick, me, axis=0)
    slot_range = jnp.arange(COUNT, dtype=jnp.int32)
    match = (slot_ids >> 3)[None, :] == owners[:, None]
    slot_of = jnp.sum(jnp.where(match, slot_range[None, :], 0), axis=1)
    cols = jnp.sum(jnp.where(match, slot_ids[None, :] & 7, 0), axis=1)
    block_of = jnp.sum(jnp.where(match, slot_range[:, None], 0), axis=0)
    info = jnp.concatenate([block_of, (slot_ids >= 0).astype(jnp.int32)])

    coarse = edge // 8
    flat = velocity[0].transpose(2, 1, 0, 3).reshape(coarse, coarse, 3 * edge).astype(bf16)
    flat = jnp.pad(flat, ((0, 0), (0, 0), (0, edge)))
    mid = jnp.pad(flat, ((0, 0), (2, 6), (0, 0)))
    edges = jnp.roll(mid, 8, axis=1)

    matrix = shape_matrix(up_taps, smooth_taps, coarse + 4)
    column_ids = np.arange(8)[:, None, None]
    x_ids = np.arange(edge)[None, :, None]
    places = x_ids == coarse * column_ids - 2 + np.arange(coarse + 4)[None, None, :]
    doubled = jnp.concatenate([matrix, matrix], axis=0).astype(bf16)
    along_x = jnp.einsum(
        "gkj,cj->gkc", places.astype(bf16), doubled, preferred_element_type=f32
    ).astype(bf16)
    padded = jnp.pad(matrix, ((0, 0), (0, 4)))
    left_v = (matrix[:8, :5][:, None, :, None] * padded[None, :, None, :]).reshape(8 * edge, 80)
    left_v = left_v.astype(bf16)

    mats = jnp.take(weights, slot_of, axis=0)
    a0, a1, a2 = (mats[:, :, d * edge : (d + 1) * edge] for d in range(3))
    a2 = jnp.concatenate([a2, a2], axis=1).transpose(0, 2, 1)
    difference = difference_matrix()
    diff_z = jnp.asarray(difference, bf16)
    diff_x = jnp.asarray(np.kron(np.eye(4, dtype=np.float32), difference.T), bf16)

    block = source.shape[1:]
    result = jax.ShapeDtypeStruct((COUNT,) + block, bf16)
    moved = jax.ShapeDtypeStruct((COUNT, 2) + block, bf16)
    cells = edge * edge
    dma = pltpu.SemaphoreType.DMA
    smem, vmem, hbm = (pl.BlockSpec(memory_space=m) for m in (pltpu.SMEM, pltpu.VMEM, pl.ANY))
    image, moment, _, _ = pl.pallas_call(
        shoot_kernel,
        out_shape=[result, result, moved, moved],
        in_specs=[smem] * 3 + [vmem] * 11,
        out_specs=[hbm] * 4,
        scratch_shapes=[
            pltpu.VMEM((COUNT, 2) + block, bf16),
            pltpu.VMEM((2, 2) + block, bf16),
            pltpu.VMEM((2,) + block, bf16),
            pltpu.VMEM((rows_x, rows_z) + mid.shape, bf16),
            pltpu.VMEM((2,) + mid.shape, bf16),
            pltpu.VMEM((192, 384), bf16),
            pltpu.VMEM((edge * PITCH, 128), f32),
            pltpu.VMEM((edge * PITCH, 128), f32),
            pltpu.VMEM((cells, 128), f32),
            pltpu.VMEM((cells, 128), f32),
            pltpu.VMEM((cells + 128, 128), f32),
            dma((COUNT, 2)),
            dma((COUNT, 2)),
            dma((COUNT, 2)),
            dma((COUNT, 2)),
            dma((14,)),
            dma((14,)),
            dma((2,)),
            dma((2,)),
        ],
        compiler_params=pltpu.CompilerParams(
            collective_id=0, has_side_effects=True, vmem_limit_bytes=58 * 1024 * 1024
        ),
        name="shoot",
    )(picks, cols, owners, source, momentum, mid, edges, along_x, a2, a1, a0, left_v, diff_z, diff_x)
    return tuple(place(info, image, moment))


def solution(mesh):
    placed = (
        P(("slab", "grp"), None, None),
        P(("slab", "grp"), None, None),
        P(None, None, "slab", "grp", None),
        P(),
        P(),
        P(("slab", "grp"), None, None),
        P("slab", None),
    )
    return jax.shard_map(
        local,
        mesh=mesh,
        in_specs=placed,
        out_specs=(P(("slab", "grp"), None, None), P(("slab", "grp"), None, None)),
        check_vma=False,
    )
```

```python
import functools

import jax
import jax.numpy as jnp
import numpy as np
from jax import lax
from jax.experimental import pallas as pl
from jax.experimental.pallas import tpu as pltpu
from jax.sharding import PartitionSpec as P

step_time = 0.5
highest = lax.Precision.HIGHEST
edge = 64
rows_z = 4
rows_x = 4
f32 = jnp.float32
bf16 = jnp.bfloat16

PITCH = 72
UNROLL = 8
MESH = pl.DeviceIdType.MESH

NEAR = ((0, 1), (0, 3), (1, 0), (3, 0))
DIAGONAL = ((1, 1), (1, 3), (3, 1), (3, 3))
CORNER = ((2, 2),)
KNIGHT = ((2, 1), (1, 2), (2, 3), (3, 2))
FAR = ((0, 2), (2, 0))
ORDER = ((0, 0),) + NEAR + DIAGONAL + CORNER + KNIGHT + FAR
COUNT = len(ORDER)


def shape_matrix(up_taps, smooth_taps, window_len):
    row_ids = jnp.arange(edge, dtype=jnp.int32)[:, None, None]
    col_ids = jnp.arange(window_len, dtype=jnp.int32)[None, :, None]
    tap_ids = jnp.arange(17, dtype=jnp.int32)[None, None, :]
    up_ids = jnp.arange(16, dtype=jnp.int32)[None, None, None, :]
    tap_index = row_ids + tap_ids - 8 * col_ids + 12
    chosen = (tap_index[..., None] == up_ids).astype(f32)
    return jnp.sum(chosen * up_taps * smooth_taps[:, None], axis=(2, 3))


def difference_matrix():
    difference = np.zeros((edge, edge), np.float32)
    for r in range(edge):
        lower, upper = max(r - 1, 0), min(r + 1, edge - 1)
        difference[r, upper] += 1.0 / (upper - lower)
        difference[r, lower] -= 1.0 / (upper - lower)
    return difference


def brick(n, in_ref, a2_ref, a1_ref, a0_ref, t_ref, l_ref, dz_ref, dx_ref, out_ref, s1, s2, s3, s4, s5):
    left = lax.broadcasted_iota(jnp.int32, (1, 128), 1) < edge

    a2 = a2_ref[n]
    none = jnp.zeros_like(a2)
    halves = [jnp.where(left, a2, none), jnp.where(left, none, a2)]
    w2 = jnp.concatenate(
        [jnp.concatenate(p, axis=1) for half in halves for p in ((half, none), (none, half))], axis=0
    )

    def x_pass(h, c):
        pieces = []
        for k in range(4):
            at = pl.ds(pl.multiple_of(h * 512 + k * 128, 128), 128)
            pieces.append(jnp.concatenate([in_ref[0, :, at], in_ref[1, :, at]], axis=1))
        res = jnp.dot(jnp.concatenate(pieces, axis=0), w2, preferred_element_type=f32)
        for k in range(4):
            for p in range(2):
                row = pl.multiple_of((h * 8 + 2 * k + p) * PITCH, 8)
                s1[pl.ds(row, 64), :] = res[k * 64 : (k + 1) * 64, p * 128 : (p + 1) * 128]
        return c

    lax.fori_loop(0, 8, x_pass, 0, unroll=UNROLL)

    def y_pass(h, c):
        cols = [s1[pl.ds(h * 8 + i, 64, stride=PITCH), :].astype(bf16) for i in range(8)]
        res = jnp.dot(a1_ref[n], jnp.concatenate(cols, axis=1), preferred_element_type=f32)
        for i in range(8):
            row = pl.multiple_of((h * 8 + i) * PITCH, 8)
            s2[pl.ds(row, 64), :] = res[:, i * 128 : (i + 1) * 128]
        return c

    lax.fori_loop(0, 8, y_pass, 0, unroll=UNROLL)

    def to_rows(x):
        return jnp.concatenate([x[:, i * 128 : (i + 1) * 128] for i in range(8)], axis=0)

    def to_cols(x):
        return jnp.concatenate([x[i * 64 : (i + 1) * 64] for i in range(8)], axis=1)

    def z_pass(h, c):
        cols = [s2[pl.ds(h * 8 + i, 64, stride=PITCH), :].astype(bf16) for i in range(8)]
        j = to_rows(
            jnp.dot(a0_ref[n], jnp.concatenate(cols, axis=1), preferred_element_type=f32)
        )
        at = pl.ds(pl.multiple_of(h * 16, 16), 80)
        v = jnp.dot(l_ref[...], t_ref[at, :], preferred_element_type=f32)
        vz, vy, vx = v[:, :128], v[:, 128:256], v[:, 256:]
        carry_z = jnp.where(left, j, vz * j).astype(bf16)
        carry_y = jnp.where(left, j, vy * j).astype(bf16)
        carry_x = jnp.where(left, j, vx * j).astype(bf16)
        gz = to_rows(jnp.dot(dz_ref[...], to_cols(carry_z), preferred_element_type=f32))
        pairs = jnp.concatenate(
            [
                jnp.concatenate(
                    [carry_x[(2 * k) * 64 : (2 * k + 1) * 64], carry_x[(2 * k + 1) * 64 : (2 * k + 2) * 64]],
                    axis=1,
                )
                for k in range(4)
            ],
            axis=0,
        )
        gp = jnp.dot(pairs, dx_ref[...], preferred_element_type=f32)
        gx = jnp.concatenate(
            [gp[k * 64 : (k + 1) * 64, p * 128 : (p + 1) * 128] for k in range(4) for p in range(2)],
            axis=0,
        )
        upd = jnp.where(left, vz, 1.0) * gz + jnp.where(left, vx, 1.0) * gx
        row = pl.multiple_of(h * 512, 512)
        s3[pl.ds(row, 512), :] = j - step_time * upd
        s4[pl.ds(row, 512), :] = (0.5 * step_time) * jnp.where(left, vy, 1.0)
        s5[pl.ds(row + 64, 512), :] = carry_y.astype(f32)
        return c

    lax.fori_loop(0, 8, z_pass, 0, unroll=UNROLL)
    s5[0:64, :] = 2.0 * s5[64:128, :] - s5[128:192, :]
    s5[65 * 64 : 66 * 64, :] = 2.0 * s5[64 * 64 : 65 * 64, :] - s5[63 * 64 : 64 * 64, :]

    def finish(h, c):
        for k in range(4):
            o = []
            for p in range(2):
                row = pl.multiple_of(h * 512 + (2 * k + p) * 64, 64)
                diff = s5[pl.ds(row + 128, 64), :] - s5[pl.ds(row, 64), :]
                o.append(s3[pl.ds(row, 64), :] - s4[pl.ds(row, 64), :] * diff)
            at = pl.ds(pl.multiple_of(h * 512 + k * 128, 128), 128)
            img = jnp.where(left, o[0], pltpu.roll(o[1], 64, 1))
            mom = jnp.where(left, pltpu.roll(o[0], 64, 1), o[1])
            out_ref[0, :, at] = img.astype(bf16)
            out_ref[1, :, at] = mom.astype(bf16)
        return c

    lax.fori_loop(0, 8, finish, 0, unroll=UNROLL)


def shoot_kernel(
    picks, cols, owners, src_ref, mom_ref, mid_ref, edge_ref, x_ref, a2_ref, a1_ref, a0_ref,
    l_ref, dz_ref, dx_ref,
    oimg_ref, omom_ref, arr_ref, inter_ref,
    stage, in_buf, out_buf, plane, halo, t_buf, s1, s2, s3, s4, s5,
    send1, recv1, send2, recv2, vsend, vrecv, in_sem, out_sem,
):
    grp, slab = lax.axis_index("grp"), lax.axis_index("slab")
    my_z, my_x = grp // rows_x, grp % rows_x
    slabs = lax.axis_size("slab")

    def at_offset(dz, dx):
        return {"slab": slab, "grp": lax.rem(my_z + dz, rows_z) * rows_x + lax.rem(my_x + dx, rows_x)}

    def at_slab(step):
        return {"slab": lax.rem(slab + step + slabs, slabs), "grp": grp}

    barrier = pltpu.get_barrier_semaphore()
    peers = [at_offset(d, 0) for d in (1, 2, 3)] + [at_offset(0, d) for d in (1, 2, 3)]
    peers += [at_slab(1), at_slab(-1)]
    for peer in peers:
        pl.semaphore_signal(barrier, inc=1, device_id=peer, device_id_type=MESH)
    pl.semaphore_wait(barrier, len(peers))

    def remote(src, dst, send, recv, device):
        return pltpu.make_async_remote_copy(
            src_ref=src, dst_ref=dst, send_sem=send, recv_sem=recv, device_id=device, device_id_type=MESH
        )

    halos = [
        remote(edge_ref, halo.at[0], vsend.at[0], vrecv.at[0], at_slab(1)),
        remote(edge_ref, halo.at[1], vsend.at[1], vrecv.at[1], at_slab(-1)),
    ]
    for c in halos:
        c.start()

    first, second = {}, {}
    for n, (dz, dx) in enumerate(ORDER):
        if n == 0:
            continue
        both = dz != 0 and dx != 0
        for f in range(2):
            leg1 = at_offset(dz, 0) if (f == 0) == (dz != 0) or dx == 0 else at_offset(0, dx)
            if not both:
                leg1 = at_offset(dz, dx)
            into = inter_ref.at[n, f] if both else arr_ref.at[n, f]
            first[n, f] = remote(stage.at[n, f], into, send1.at[n, f], recv1.at[n, f], leg1)
            if both:
                leg2 = at_offset(0, dx) if f == 0 else at_offset(dz, 0)
                second[n, f] = remote(
                    inter_ref.at[n, f], arr_ref.at[n, f], send2.at[n, f], recv2.at[n, f], leg2
                )

    def put(n, c):
        stage[n, 0] = src_ref[picks[n]]
        stage[n, 1] = mom_ref[picks[n]]
        return c

    def start(copies, ns):
        for n in ns:
            for f in range(2):
                copies[n, f].start()

    def landed(copies, ns):
        for n in ns:
            for f in range(2):
                copies[n, f].wait_recv()

    near, diagonal, corner, knight = range(1, 5), range(5, 9), [9], range(10, 14)
    for group in (near, diagonal, knight):
        lax.fori_loop(group[0], group[-1] + 1, put, 0)
        start(first, group)

    for c in halos:
        c.wait()
    piece = mid_ref[...]
    layer = lax.broadcasted_iota(jnp.int32, piece.shape, 1)
    below = (layer < 2) & (slab > 0)
    above = (layer >= 10) & (layer < 12) & (slab < slabs - 1)
    plane[my_x, my_z] = jnp.where(below, halo[0], jnp.where(above, halo[1], piece))
    lower, upper = pl.ds(0, 4), pl.ds(4, 4)
    mine_lower, mine_upper = plane.at[my_x, my_z, lower], plane.at[my_x, my_z, upper]
    leg1 = [remote(mine_lower, mine_lower, vsend.at[1 + d], vrecv.at[1 + d], at_offset(d, 0)) for d in (1, 2, 3)]
    leg1 += [remote(mine_upper, mine_upper, vsend.at[4 + d], vrecv.at[4 + d], at_offset(0, d)) for d in (1, 2, 3)]
    for c in leg1:
        c.start()
    lax.fori_loop(9, 10, put, 0)
    lax.fori_loop(14, 16, put, 0)
    for c in leg1:
        c.wait()
    row_lower, row_upper = plane.at[my_x, :, lower], plane.at[:, my_z, upper]
    leg2 = [remote(row_lower, row_lower, vsend.at[7 + d], vrecv.at[7 + d], at_offset(0, d)) for d in (1, 2, 3)]
    leg2 += [remote(row_upper, row_upper, vsend.at[10 + d], vrecv.at[10 + d], at_offset(d, 0)) for d in (1, 2, 3)]
    for c in leg2:
        c.start()
    lax.fori_loop(0, 1, put, 0)
    for c in leg2:
        c.wait()

    def window(n):
        owner, last = owners[n], rows_z * rows_x - 1
        before, after = jnp.maximum(owner - 1, 0), jnp.minimum(owner + 1, last)
        pieces = [
            plane[before & 3, before >> 2, 6:8].reshape(32, 256),
            plane[owner & 3, owner >> 2].reshape(128, 256),
            plane[after & 3, after >> 2, 0:2].reshape(32, 256),
        ]
        pieces[0] = jnp.where(owner > 0, pieces[0], jnp.zeros_like(pieces[0]))
        pieces[2] = jnp.where(owner < last, pieces[2], jnp.zeros_like(pieces[2]))
        w = jnp.concatenate(pieces, axis=0)
        along = x_ref[cols[n]]
        none = jnp.zeros_like(along)
        upper = jnp.concatenate([along, none], axis=0)
        paired = jnp.concatenate([upper, jnp.concatenate([none, along], axis=0)], axis=1)
        t_buf[:, :256] = jnp.dot(w[:, :128], paired, preferred_element_type=f32).astype(bf16)
        t_buf[:, 256:] = jnp.dot(w[:, 128:], upper, preferred_element_type=f32).astype(bf16)

    def results(n):
        return [
            pltpu.make_async_copy(out_buf.at[f], ref.at[n], out_sem.at[f])
            for f, ref in enumerate((oimg_ref, omom_ref))
        ]

    def before_near():
        landed(first, diagonal)
        start(second, diagonal)
        start(first, corner)
        landed(first, near)

    def before_diagonal():
        landed(first, knight)
        start(second, knight)
        landed(first, corner)
        start(second, corner)
        landed(second, diagonal)

    def before_corner():
        landed(second, corner)
        start(first, [14, 15])

    hooks = {
        1: before_near,
        5: before_diagonal,
        9: before_corner,
        10: lambda: landed(second, knight[:2]),
        12: lambda: landed(second, knight[2:]),
        14: lambda: landed(first, [14]),
        15: lambda: landed(first, [15]),
    }

    def fetch(n):
        return pltpu.make_async_copy(arr_ref.at[n], in_buf.at[n % 2], in_sem.at[n % 2])

    def work(n, c):
        for at, hook in hooks.items():
            pl.when(n == at)(hook)

        opens, ends = n < 0, n == COUNT - 1
        for at in (1, 5, 9, 10, 12, 14, 15):
            opens = opens | (n == at)
            ends = ends | (n == at - 1)

        @pl.when(n == 0)
        def _():
            in_buf[0] = stage[0]

        @pl.when(opens)
        def _():
            fetch(n).start()

        window(n)

        @pl.when(n > 0)
        def _():
            for done in results(n - 1):
                done.wait()
            fetch(n).wait()

        @pl.when(jnp.logical_not(ends))
        def _():
            fetch(n + 1).start()

        brick(
            n, in_buf.at[n % 2], a2_ref, a1_ref, a0_ref, t_buf, l_ref, dz_ref, dx_ref, out_buf, s1, s2, s3, s4, s5
        )
        for out in results(n):
            out.start()
        return c

    lax.fori_loop(0, COUNT, work, 0)
    for done in results(COUNT - 1):
        done.wait()
    for copies in (first, second):
        for c in copies.values():
            c.wait_send()


def place_kernel(info, img_ref, mom_ref, oimg_ref, omom_ref, held, zeros, in_sem, out_sem):
    fields = ((img_ref, oimg_ref), (mom_ref, omom_ref))

    def read(j, f):
        return pltpu.make_async_copy(fields[f][0].at[info[j]], held.at[j, f], in_sem.at[j, f])

    def write(j, f, source):
        return pltpu.make_async_copy(source, fields[f][1].at[j], out_sem.at[j, f])

    def begin(j, c):
        @pl.when(info[COUNT + j] != 0)
        def _():
            read(j, 0).start()
            read(j, 1).start()

        return c

    lax.fori_loop(0, COUNT, begin, 0)
    zeros[...] = jnp.zeros_like(zeros)

    def move(j, c):
        @pl.when(info[COUNT + j] != 0)
        def _():
            for f in range(2):
                read(j, f).wait()
                write(j, f, held.at[j, f]).start()

        @pl.when(info[COUNT + j] == 0)
        def _():
            for f in range(2):
                write(j, f, zeros).start()

        return c

    lax.fori_loop(0, COUNT, move, 0)

    def end(j, c):
        for f in range(2):
            write(j, f, zeros).wait()
        return c

    lax.fori_loop(0, COUNT, end, 0)


def place(info, image, moment):
    block = image.shape[1:]
    hbm = pl.BlockSpec(memory_space=pl.ANY)
    return pl.pallas_call(
        place_kernel,
        grid_spec=pltpu.PrefetchScalarGridSpec(
            num_scalar_prefetch=1,
            grid=(1,),
            in_specs=[hbm] * 2,
            out_specs=[hbm] * 2,
            scratch_shapes=[
                pltpu.VMEM((COUNT, 2) + block, bf16),
                pltpu.VMEM(block, bf16),
                pltpu.SemaphoreType.DMA((COUNT, 2)),
                pltpu.SemaphoreType.DMA((COUNT, 2)),
            ],
        ),
        out_shape=[jax.ShapeDtypeStruct(image.shape, image.dtype)] * 2,
        compiler_params=pltpu.CompilerParams(vmem_limit_bytes=60 * 1024 * 1024),
        name="place",
    )(info, image, moment)


def local(source, momentum, velocity, up_taps, smooth_taps, weights, slot_brick):
    me = lax.axis_index("grp")
    my_z, my_x = me // rows_x, me % rows_x
    off_z = jnp.array([o[0] for o in ORDER], jnp.int32)
    off_x = jnp.array([o[1] for o in ORDER], jnp.int32)
    targets = ((my_z + off_z) % rows_z) * rows_x + (my_x + off_x) % rows_x
    owners = ((my_z - off_z) % rows_z) * rows_x + (my_x - off_x) % rows_x
    rows = jnp.take(slot_brick, targets, axis=0)
    picks = jnp.sum(jnp.where((rows >> 3) == me, rows & 7, 0), axis=1)

    slot_ids = jnp.take(slot_brick, me, axis=0)
    slot_range = jnp.arange(COUNT, dtype=jnp.int32)
    match = (slot_ids >> 3)[None, :] == owners[:, None]
    slot_of = jnp.sum(jnp.where(match, slot_range[None, :], 0), axis=1)
    cols = jnp.sum(jnp.where(match, slot_ids[None, :] & 7, 0), axis=1)
    block_of = jnp.sum(jnp.where(match, slot_range[:, None], 0), axis=0)
    info = jnp.concatenate([block_of, (slot_ids >= 0).astype(jnp.int32)])

    coarse = edge // 8
    flat = velocity[0].transpose(2, 1, 0, 3).reshape(coarse, coarse, 3 * edge).astype(bf16)
    flat = jnp.pad(flat, ((0, 0), (0, 0), (0, edge)))
    mid = jnp.pad(flat, ((0, 0), (2, 6), (0, 0)))
    edges = jnp.roll(mid, 8, axis=1)

    matrix = shape_matrix(up_taps, smooth_taps, coarse + 4)
    column_ids = np.arange(8)[:, None, None]
    x_ids = np.arange(edge)[None, :, None]
    places = x_ids == coarse * column_ids - 2 + np.arange(coarse + 4)[None, None, :]
    doubled = jnp.concatenate([matrix, matrix], axis=0).astype(bf16)
    along_x = jnp.einsum(
        "gkj,cj->gkc", places.astype(bf16), doubled, preferred_element_type=f32
    ).astype(bf16)
    padded = jnp.pad(matrix, ((0, 0), (0, 4)))
    left_v = (matrix[:8, :5][:, None, :, None] * padded[None, :, None, :]).reshape(8 * edge, 80)
    left_v = left_v.astype(bf16)

    mats = jnp.take(weights, slot_of, axis=0)
    a0, a1, a2 = (mats[:, :, d * edge : (d + 1) * edge] for d in range(3))
    a2 = jnp.concatenate([a2, a2], axis=1).transpose(0, 2, 1)
    difference = difference_matrix()
    diff_z = jnp.asarray(difference, bf16)
    diff_x = jnp.asarray(np.kron(np.eye(4, dtype=np.float32), difference.T), bf16)

    block = source.shape[1:]
    result = jax.ShapeDtypeStruct((COUNT,) + block, bf16)
    moved = jax.ShapeDtypeStruct((COUNT, 2) + block, bf16)
    cells = edge * edge
    dma = pltpu.SemaphoreType.DMA
    smem, vmem, hbm = (pl.BlockSpec(memory_space=m) for m in (pltpu.SMEM, pltpu.VMEM, pl.ANY))
    image, moment, _, _ = pl.pallas_call(
        shoot_kernel,
        out_shape=[result, result, moved, moved],
        in_specs=[smem] * 3 + [vmem] * 11,
        out_specs=[hbm] * 4,
        scratch_shapes=[
            pltpu.VMEM((COUNT, 2) + block, bf16),
            pltpu.VMEM((2, 2) + block, bf16),
            pltpu.VMEM((2,) + block, bf16),
            pltpu.VMEM((rows_x, rows_z) + mid.shape, bf16),
            pltpu.VMEM((2,) + mid.shape, bf16),
            pltpu.VMEM((192, 384), bf16),
            pltpu.VMEM((edge * PITCH, 128), f32),
            pltpu.VMEM((edge * PITCH, 128), f32),
            pltpu.VMEM((cells, 128), f32),
            pltpu.VMEM((cells, 128), f32),
            pltpu.VMEM((cells + 128, 128), f32),
            dma((COUNT, 2)),
            dma((COUNT, 2)),
            dma((COUNT, 2)),
            dma((COUNT, 2)),
            dma((14,)),
            dma((14,)),
            dma((2,)),
            dma((2,)),
        ],
        compiler_params=pltpu.CompilerParams(
            collective_id=0, has_side_effects=True, vmem_limit_bytes=58 * 1024 * 1024
        ),
        name="shoot",
    )(picks, cols, owners, source, momentum, mid, edges, along_x, a2, a1, a0, left_v, diff_z, diff_x)
    return tuple(place(info, image, moment))


def solution(mesh):
    placed = (
        P(("slab", "grp"), None, None),
        P(("slab", "grp"), None, None),
        P(None, None, "slab", "grp", None),
        P(),
        P(),
        P(("slab", "grp"), None, None),
        P("slab", None),
    )
    return jax.shard_map(
        local,
        mesh=mesh,
        in_specs=placed,
        out_specs=(P(("slab", "grp"), None, None), P(("slab", "grp"), None, None)),
        check_vma=False,
    )
```
